32 devices in a mesh: grp: 2 (over x), row: 16 (over z, y, core).
Axes of the slice: x: 2, y: 2, z: 4, core: 2. Of those that a mesh axis runs over, the one named last changes fastest.
Arguments:
- vis_values: bfloat16 [2, 32768], P(None, ('grp', 'row')), parts along dimension 1, may hold values from -6 to 6
- tile_row: int32 [32768], P(('grp', 'row')), parts along dimension 0, may hold values from 0 to 15, as said below
- tile_col: int32 [32768], P(('grp', 'row')), parts along dimension 0, may hold values from 0 to 1
- row_offset: int32 [32768], P(('grp', 'row')), parts along dimension 0, may hold values from 0 to 127
- col_offset: int32 [32768], P(('grp', 'row')), parts along dimension 0, may hold values from 0 to 127
- plane: int32 [32768], P(('grp', 'row')), parts along dimension 0, may hold values from 0 to 7
- plane_w: float32 [16], P('grp'), parts along dimension 0, may hold values from -1000 to 1000
Outputs:
- dirty: float32 [512, 1024], P(('grp', 'row')), parts along dimension 0
The draws below stay inside these ranges and needn't reach their ends.
There are 2 independent parts, one for each index of `grp`. The reference program is written for one: setup_inputs(seed, part) draws one part's arguments, and reference() takes and returns one part's arrays. A program takes and returns all parts, laid end to end along the dimension named above; each array names one. Nothing has to cross between parts.
Inputs may be any that keep to these rules, and one draw needn't show every extreme that they name: `tile_row`: in each device's block of 1024 visibilities no tile row is named more than 256 times; one tile row, the same for every device of a part, is named exactly 256 times in every block.
All inputs are finite; a program needn't handle non-finite values.
Results may differ from the reference program's by a relative error of at most 0.006.
Values may be sent and summed in bfloat16 or wider, within the bound.
A program may use at most 128 MiB of HBM per device.

```python
import math
import jax
import jax.numpy as jnp
from jax import lax

G = 32768
W = 8
TILE = 128
V_TILES = 2
VIS_DEV = 1024
L_OUT = 1024
M_DEV = 16
U_START = 8192
V_START = 8192
V_WIN = 256
U_WIN = 2048
M_OUT = 256
L_STEP = 33
M_STEP = 129
VIS = 16384
CAP = 256
N_ROW = 16


def draw_tile_row(key, part):
    key = jax.random.fold_in(key, 7)
    key_heavy, key_jitter, key_shift, key_order = jax.random.split(key, 4)
    heavy = jax.random.randint(key_heavy, (), 0, N_ROW)
    others = max(N_ROW - 1, 1)
    spare = VIS_DEV - CAP
    counter = jnp.arange(spare, dtype=jnp.int32)
    jitter = jax.random.randint(key_jitter, (N_ROW, spare), 0, 2)
    shift = jax.random.randint(key_shift, (N_ROW, 1), 0, others)
    chosen = (heavy + 1 + (counter[None, :] + jitter + shift) % others) % N_ROW
    heavy_rows = jnp.zeros((N_ROW, CAP), jnp.int32) + heavy
    block = jnp.concatenate([heavy_rows, chosen.astype(jnp.int32)], axis=1)
    order_keys = jax.random.split(key_order, N_ROW)
    block = jax.vmap(jax.random.permutation)(order_keys, block)
    return block.reshape(-1).astype(jnp.int32)


def plant(values, stream_key, low, high):
    shape = values.shape
    place = [jax.random.randint(jax.random.fold_in(stream_key, axis), (), 0, shape[axis]) for axis in range(len(shape))]
    values = values.at[tuple(place)].set(low)
    longest = shape.index(max(shape))
    place[longest] = (place[longest] + 1) % shape[longest]
    return values.at[tuple(place)].set(high)


def steps_of(rng, dims, pieces, least, top_value):
    def one(axis_at, blocks):
        steps = jax.random.uniform(jax.random.fold_in(jax.random.fold_in(rng, 6), axis_at), (blocks,), jnp.float32, least / len(pieces), top_value / len(pieces))
        return jnp.repeat(jnp.exp(steps), dims[axis_at] // blocks).reshape((-1,) + (1,) * (len(dims) - axis_at - 1))

    loudness = one(*pieces[0])
    for cut in pieces[1:]:
        loudness = loudness * one(*cut)
    return loudness


def scatter_about(stream_key, dims, width, most, shards=(), kind=jnp.bfloat16):
    factor_of = steps_of(stream_key, dims, shards, -0.22, 0.18) if shards else 1.0
    drawn = jax.random.normal(stream_key, dims, jnp.float32) * width * factor_of
    return jnp.minimum(jnp.maximum(drawn, -most), most).astype(kind)


def setup_inputs(seed: int = 0, part: int = 0) -> dict:
    arg_keys = jax.random.split(jax.random.key(seed), 8)
    part_splits = jax.random.split(jax.random.fold_in(arg_keys[7], part), 8)
    vis_values = scatter_about(part_splits[0], (2, VIS), 1.0, 6.0, ((1, 16),))
    tile_row = draw_tile_row(jax.random.fold_in(jax.random.fold_in(arg_keys[7], part), 71), part)
    tile_col = plant(jax.random.randint(part_splits[2], (VIS,), 0, V_TILES), jax.random.fold_in(part_splits[2], 1), 0, V_TILES - 1).astype(jnp.int32)
    row_offset = plant(jax.random.randint(part_splits[3], (VIS,), 0, TILE), jax.random.fold_in(part_splits[3], 1), 0, TILE - 1).astype(jnp.int32)
    col_offset = plant(jax.random.randint(part_splits[4], (VIS,), 0, TILE), jax.random.fold_in(part_splits[4], 1), 0, TILE - 1).astype(jnp.int32)
    plane = plant(jax.random.randint(part_splits[5], (VIS,), 0, W), jax.random.fold_in(part_splits[5], 1), 0, W - 1).astype(jnp.int32)
    plane_w = jnp.clip(jax.random.uniform(part_splits[6], (W,), jnp.float32, -1000.0, 1000.0), -1000.0, 1000.0)
    return {"vis_values": vis_values, "tile_row": tile_row, "tile_col": tile_col, "row_offset": row_offset, "col_offset": col_offset, "plane": plane, "plane_w": plane_w}


def taper(offset):
    spread = offset.astype(jnp.float32)
    inside = jnp.abs(offset) <= 4
    return jnp.where(inside, jnp.exp(-spread * spread / 8.0), jnp.float32(0.0))

def pixel_offset(index, step):
    return index * step % G - G // 2

def phase_table(along_a, along_b):
    turns = along_a[:, None] * along_b[None, :] % G
    angle = turns.astype(jnp.float32) * jnp.float32(2.0 * math.pi / G)
    return (jnp.cos(angle), jnp.sin(angle))

def screen_phase(plane_w, along_m, along_l):
    ratio_m = along_m.astype(jnp.float32) / jnp.float32(G)
    ratio_l = along_l.astype(jnp.float32) / jnp.float32(G)
    square = ratio_m[:, None] * ratio_m[:, None] + ratio_l[None, :] * ratio_l[None, :]
    lowered = square / (1.0 + jnp.sqrt(1.0 - square))
    return jnp.float32(-2.0 * math.pi) * plane_w[:, None, None] * lowered[None, :, :]

def reference(vis_values, tile_row, tile_col, row_offset, col_offset, plane, plane_w):
    values = vis_values.astype(jnp.float32)
    columns = jnp.arange(V_WIN, dtype=jnp.int32)
    relative = columns[None, :] - tile_col[:, None] * TILE - col_offset[:, None]
    same_tile = columns[None, :] // TILE == tile_col[:, None]
    kernel_cols = jnp.where(same_tile, taper(relative), jnp.float32(0.0))
    weighted = (values.T[:, :, None] * kernel_cols[:, None, :]).astype(jnp.bfloat16)
    weighted = lax.optimization_barrier(weighted).astype(jnp.float32).reshape(VIS, 2 * V_WIN)
    grid = jnp.zeros((W * U_WIN, 2 * V_WIN), jnp.float32)
    for tap_step in range(-4, 5):
        target = row_offset + tap_step
        valid = (target >= 0) & (target < TILE)
        weight_tap = taper(jnp.asarray(tap_step, jnp.int32)).astype(jnp.bfloat16)
        weight_tap = lax.optimization_barrier(weight_tap).astype(jnp.float32)
        factor = jnp.where(valid, weight_tap, jnp.float32(0.0))
        rows = plane * U_WIN + tile_row * TILE + jnp.clip(target, 0, TILE - 1)
        grid = grid.at[rows].add(weighted * factor[:, None])
    grid_low = grid.astype(jnp.bfloat16)
    along_v = V_START + jnp.arange(V_WIN, dtype=jnp.int32)
    out_rows = jnp.arange(M_OUT, dtype=jnp.int32)
    column_index = out_rows % M_DEV * N_ROW + out_rows // M_DEV
    along_m = pixel_offset(column_index, M_STEP)
    cos_v, sin_v = phase_table(along_v, along_m)
    upper = jnp.concatenate([cos_v, sin_v], axis=1)
    lower = jnp.concatenate([-sin_v, cos_v], axis=1)
    table_v = jnp.concatenate([upper, lower], axis=0).astype(jnp.bfloat16)
    partial_value = jnp.dot(grid_low, table_v, preferred_element_type=jnp.float32).astype(jnp.bfloat16)
    partial_value = partial_value.reshape(W, U_WIN, 2 * M_OUT)
    along_u = U_START + jnp.arange(U_WIN, dtype=jnp.int32)
    along_l = pixel_offset(jnp.arange(L_OUT, dtype=jnp.int32), L_STEP)
    cos_u, sin_u = phase_table(along_u, along_l)
    table_u = jnp.concatenate([cos_u, sin_u], axis=1).astype(jnp.bfloat16)
    phase = screen_phase(plane_w, along_m, along_l)

    def one_plane(total, inputs):
        plane_part, plane_phase = inputs
        mixed = lax.dot_general(plane_part.astype(jnp.float32), table_u.astype(jnp.float32), (((0,), (0,)), ((), ())), preferred_element_type=jnp.float32)
        mixed = mixed.reshape(2, M_OUT, 2, L_OUT)
        real_part = mixed[0, :, 0] - mixed[1, :, 1]
        imag_part = mixed[0, :, 1] + mixed[1, :, 0]
        total = total + jnp.cos(plane_phase) * real_part - jnp.sin(plane_phase) * imag_part
        return (total, None)
    total, unused = lax.scan(one_plane, jnp.zeros((M_OUT, L_OUT), jnp.float32), (partial_value, phase))
    return total / jnp.sqrt(jnp.float32(VIS))
```

```python
import functools
import math

import jax
import jax.numpy as jnp
from jax import lax
from jax.experimental import pallas as pl
from jax.experimental.pallas import tpu as pltpu
from jax.sharding import PartitionSpec as P

G = 32768
W = 8
TILE = 128
L_OUT = 1024
M_DEV = 16
U_START = 8192
V_START = 8192
V_WIN = 256
F32 = jnp.float32
BF16 = jnp.bfloat16
I32 = jnp.int32
NT = (((1,), (1,)), ((), ()))
SINE = [(-1) ** k * (2.0 * math.pi) ** (2 * k + 1) / math.factorial(2 * k + 1) for k in range(6)]


def quarter_sine(s):
    square = s * s
    total = jnp.full_like(s, SINE[5])
    for k in range(4, -1, -1):
        total = total * square + SINE[k]
    return total * s


def cos_turns(t):
    return quarter_sine(0.25 - jnp.abs(t))


def sin_turns(t):
    return quarter_sine(jnp.abs(jnp.abs(t - 0.25) - 0.5) - 0.25)


def wrap(turns):
    return (((turns + G // 2) & (G - 1)) - G // 2).astype(F32) * (1.0 / G)


def iota(shape, axis):
    return lax.broadcasted_iota(I32, shape, axis)


def pixel(index, step):
    return ((index * step) & (G - 1)) - G // 2


def taper(spread):
    return jnp.where(jnp.abs(spread) <= 4.0, jnp.exp(spread * spread * -0.125), 0.0)


def kernel(
    devices, cap, group, width, per_device,
    data_ref, w_ref, out_ref,
    key_s, send1, recv1, a_s, b_s, grid_s, tv_s, send2, recv2, tab_s, e1c, e1s, e2c, e2s, scr_c, scr_s,
    ss1, rs1, ss2, rs2,
):
    me = lax.axis_index("row")
    blocks = devices // group
    m_step = G // (M_DEV * devices) + 1
    l_step = G // L_OUT + 1
    barrier = pltpu.get_barrier_semaphore()

    def greet(i, carry):
        pl.semaphore_signal(
            barrier, inc=1, device_id={"row": lax.rem(me + i, devices)},
            device_id_type=pl.DeviceIdType.MESH,
        )
        return carry

    lax.fori_loop(1, devices, greet, 0)

    def copy1(i):
        peer = lax.rem(me + i, devices)
        return pltpu.make_async_remote_copy(
            src_ref=send1.at[peer], dst_ref=recv1.at[me], send_sem=ss1.at[i], recv_sem=rs1.at[i],
            device_id={"row": peer}, device_id_type=pl.DeviceIdType.MESH,
        )

    def arrive1(i):
        source = lax.rem(me - i + devices, devices)
        return pltpu.make_async_remote_copy(
            src_ref=send1.at[source], dst_ref=recv1.at[source], send_sem=ss1.at[i], recv_sem=rs1.at[i],
            device_id={"row": source}, device_id_type=pl.DeviceIdType.MESH,
        )

    def copy2(i):
        peer = lax.rem(me + i, devices)
        return pltpu.make_async_remote_copy(
            src_ref=send2.at[peer], dst_ref=recv2.at[me], send_sem=ss2.at[i], recv_sem=rs2.at[i],
            device_id={"row": peer}, device_id_type=pl.DeviceIdType.MESH,
        )

    def arrive2(i):
        source = lax.rem(me - i + devices, devices)
        return pltpu.make_async_remote_copy(
            src_ref=send2.at[source], dst_ref=recv2.at[source], send_sem=ss2.at[i], recv_sem=rs2.at[i],
            device_id={"row": source}, device_id_type=pl.DeviceIdType.MESH,
        )

    with jax.named_scope("pack"):
        data = data_ref[...]
        member = jnp.where(data[6:7, :] == iota((devices, per_device), 0).astype(F32), 1.0, 0.0)
        parts = [member[:, c * 128 : (c + 1) * 128] for c in range(per_device // 128)]
        below = jnp.where(iota((128, 128), 0) < iota((128, 128), 1), 1.0, 0.0).astype(BF16)
        ranks = jnp.dot(jnp.concatenate(parts, axis=0).astype(BF16), below, preferred_element_type=F32)
        before = jnp.zeros((devices, 1), F32) + lax.rem(me, group).astype(F32) * cap
        for c, part in enumerate(parts):
            rank = ranks[c * devices : (c + 1) * devices] + before
            key_s[:, c * 128 : (c + 1) * 128] = jnp.where(part > 0.0, rank, -1.0)
            before = before + jnp.sum(part, axis=1, keepdims=True)
        low = data.astype(BF16)

        def packed(d):
            slot = iota((width, per_device), 0).astype(F32)
            hot = jnp.where(slot == key_s[pl.ds(d, 1), :], 1.0, 0.0).astype(BF16)
            return lax.dot_general(low, hot, NT, preferred_element_type=F32)

        pl.semaphore_wait(barrier, devices - 1)

        def send_block(i, carry):
            d = lax.rem(me + i, devices)
            send1[d] = packed(d)
            copy1(i).start()
            return carry

        lax.fori_loop(1, devices, send_block, 0)
        recv1[me] = packed(me)

    with jax.named_scope("tables"):
        rows = 2 * M_DEV * devices
        tile_rows = 256

        def table_v(k, carry):
            row = iota((tile_rows, V_WIN), 0) + k * tile_rows
            owner = row >> 5
            part = (row >> 4) & 1
            om = pixel((row & 15) * devices + owner, m_step)
            turns = (iota((tile_rows, V_WIN), 1) + V_START) * om
            at = pl.ds(pl.multiple_of(k * tile_rows, tile_rows), tile_rows)
            tv_s[at, :V_WIN] = cos_turns(wrap(turns - part * (G // 4))).astype(BF16)
            tv_s[at, V_WIN:] = cos_turns(wrap(turns + (1 - part) * (G // 4))).astype(BF16)
            return carry

        lax.fori_loop(0, rows // tile_rows, table_v, 0)
        ol = pixel(iota((TILE, L_OUT), 1), l_step)
        turn2 = wrap(iota((TILE, L_OUT), 0) * ol)
        e2c[...] = cos_turns(turn2)
        e2s[...] = sin_turns(turn2)
        ol1 = pixel(iota((devices, L_OUT), 1), l_step)
        turn1 = wrap((iota((devices, L_OUT), 0) * TILE + U_START) * ol1)
        e1c[...] = cos_turns(turn1)
        e1s[...] = sin_turns(turn1)

    def wait1(i, carry):
        arrive1(i).wait_recv()
        return carry

    lax.fori_loop(1, devices, wait1, 0)

    with jax.named_scope("spread"):

        def spread(k, carry):
            block = recv1[k * group]
            for j in range(1, group):
                block = block + recv1[k * group + j]
            at = pl.ds(pl.multiple_of(k * width, width), width)
            down = iota((TILE, width), 0).astype(F32)
            rows_k = taper(down - block[3:4, :]).astype(BF16)
            for p in range(W):
                mask = jnp.where(block[2:3, :] == p + 1.0, 1.0, 0.0).astype(BF16)
                b_s[p * TILE : (p + 1) * TILE, at] = rows_k * mask
            cols_k = taper(down - block[5:6, :])
            for e in range(2):
                for h in range(2):
                    value = jnp.where(block[4:5, :] == float(h), block[e : e + 1, :], 0.0)
                    first = e * V_WIN + h * TILE
                    a_s[first : first + TILE, at] = (cols_k * value).astype(BF16)
            return carry

        lax.fori_loop(0, blocks, spread, 0)

    with jax.named_scope("gridding"):

        def grid_tile(j, carry):
            at = pl.ds(pl.multiple_of(j * 256, 256), 256)
            grid_s[:, at] = lax.dot_general(a_s[...], b_s[at, :], NT, preferred_element_type=F32).astype(BF16)
            return carry

        lax.fori_loop(0, W * TILE // 256, grid_tile, 0)

    with jax.named_scope("columns"):
        per_step = 8

        def columns(k, carry):
            at = pl.ds(pl.multiple_of(k * 32 * per_step, 32 * per_step), 32 * per_step)
            block = jnp.dot(tv_s[at, :], grid_s[...], preferred_element_type=F32).astype(BF16)
            for j in range(per_step):
                send2[k * per_step + j] = block[j * 32 : (j + 1) * 32]
            return carry

        lax.fori_loop(0, devices // per_step, columns, 0)

        def start2(i, carry):
            copy2(i).start()
            return carry

        lax.fori_loop(1, devices, start2, 0)
        recv2[me] = send2[me]

    with jax.named_scope("row_table"):

        def table_u(s, carry):
            at = pl.ds(pl.multiple_of(s * TILE, TILE), TILE)
            c1, s1 = e1c[pl.ds(s, 1), :], e1s[pl.ds(s, 1), :]
            c2, s2 = e2c[...], e2s[...]
            tab_s[at, :L_OUT] = (c1 * c2 - s1 * s2).astype(BF16)
            tab_s[at, L_OUT:] = (s1 * c2 + c1 * s2).astype(BF16)
            return carry

        lax.fori_loop(0, devices, table_u, 0)

    with jax.named_scope("screen"):
        scale = 1.0 / math.sqrt(per_device * devices)
        y = pixel(iota((M_DEV, L_OUT), 0) * devices + me, m_step).astype(F32) * (1.0 / G)
        x = pixel(iota((M_DEV, L_OUT), 1), l_step).astype(F32) * (1.0 / G)
        q = x * x + y * y
        lowered = q / (1.0 + jnp.sqrt(1.0 - q))
        for p in range(W):
            turns = lowered * -w_ref[p]
            turns = turns - jnp.floor(turns + 0.5)
            scr_c[p] = cos_turns(turns) * scale
            scr_s[p] = sin_turns(turns) * scale

    def wait2(i, carry):
        arrive2(i).wait_recv()
        return carry

    lax.fori_loop(1, devices, wait2, 0)

    with jax.named_scope("rows"):

        depth = min(TILE * devices, b_s.shape[1])
        turns_k = TILE * devices // depth
        for h in range(turns_k):

            def regroup(s, carry):
                at = pl.ds(pl.multiple_of(s * TILE, TILE), TILE)
                for p in range(W):
                    first = h * 32 * W + p * 32
                    b_s[first : first + 32, at] = recv2[s + h * (depth // TILE), :, p * TILE : (p + 1) * TILE]
                return carry

            lax.fori_loop(0, depth // TILE, regroup, 0)

        def rows_by(at):
            total = None
            for h in range(turns_k):
                left = b_s[h * 32 * W : (h + 1) * 32 * W, :depth]
                right = tab_s[h * depth : (h + 1) * depth, at]
                part = jnp.dot(left, right, preferred_element_type=F32)
                total = part if total is None else total + part
            return total

        def image(k, carry):
            at = pl.ds(pl.multiple_of(k * 256, 256), 256)
            also = pl.ds(pl.multiple_of(k * 256 + L_OUT, 256), 256)
            by_cos = rows_by(at)
            by_sin = rows_by(also)
            total = jnp.zeros((M_DEV, 256), F32)
            for p in range(W):
                r0, r1, r2 = p * 32, p * 32 + 16, p * 32 + 32
                real = by_cos[r0:r1] - by_sin[r1:r2]
                imag = by_sin[r0:r1] + by_cos[r1:r2]
                total = total + scr_c[p, :, at] * real - scr_s[p, :, at] * imag
            out_ref[:, at] = total
            return carry

        lax.fori_loop(0, L_OUT // 256, image, 0)

    def drain(i, carry):
        copy1(i).wait_send()
        copy2(i).wait_send()
        return carry

    lax.fori_loop(1, devices, drain, 0)


def on_device(vis_values, tile_row, tile_col, row_offset, col_offset, plane, plane_w):
    devices = lax.axis_size("row")
    per_device = vis_values.shape[1]
    cap = 4 * per_device // devices
    group = max(1, 128 // cap)
    width = cap * group
    slots = width * (devices // group)
    ints = jnp.stack([plane + 1, row_offset, tile_col, col_offset, tile_row, jnp.zeros_like(plane)])
    data = jnp.concatenate([vis_values.astype(F32), ints.astype(F32)], axis=0)
    vmem = pl.BlockSpec(memory_space=pltpu.VMEM)
    return pl.pallas_call(
        functools.partial(kernel, devices, cap, group, width, per_device),
        out_shape=jax.ShapeDtypeStruct((M_DEV, L_OUT), F32),
        in_specs=[vmem, pl.BlockSpec(memory_space=pltpu.SMEM)],
        out_specs=vmem,
        scratch_shapes=[
            pltpu.VMEM((devices, per_device), F32),
            pltpu.VMEM((devices, 8, width), F32),
            pltpu.VMEM((devices, 8, width), F32),
            pltpu.VMEM((2 * V_WIN, slots), BF16),
            pltpu.VMEM((W * TILE, slots), BF16),
            pltpu.VMEM((2 * V_WIN, W * TILE), BF16),
            pltpu.VMEM((2 * M_DEV * devices, 2 * V_WIN), BF16),
            pltpu.VMEM((devices, 2 * M_DEV, W * TILE), BF16),
            pltpu.VMEM((devices, 2 * M_DEV, W * TILE), BF16),
            pltpu.VMEM((TILE * devices, 2 * L_OUT), BF16),
            pltpu.VMEM((devices, L_OUT), F32),
            pltpu.VMEM((devices, L_OUT), F32),
            pltpu.VMEM((TILE, L_OUT), F32),
            pltpu.VMEM((TILE, L_OUT), F32),
            pltpu.VMEM((W, M_DEV, L_OUT), F32),
            pltpu.VMEM((W, M_DEV, L_OUT), F32),
            pltpu.SemaphoreType.DMA((devices,)),
            pltpu.SemaphoreType.DMA((devices,)),
            pltpu.SemaphoreType.DMA((devices,)),
            pltpu.SemaphoreType.DMA((devices,)),
        ],
        compiler_params=pltpu.CompilerParams(
            collective_id=0, has_side_effects=True, vmem_limit_bytes=(32 if devices <= 16 else 62) * 2**20
        ),
    )(data, plane_w)


def solution(mesh):
    vector = P(("grp", "row"))
    in_specs = (P(None, ("grp", "row")), vector, vector, vector, vector, vector, P("grp"))
    return jax.shard_map(
        on_device, mesh=mesh, in_specs=in_specs, out_specs=P(("grp", "row"), None), check_vma=False
    )
```

```python
import functools
import math

import jax
import jax.numpy as jnp
from jax import lax
from jax.experimental import pallas as pl
from jax.experimental.pallas import tpu as pltpu
from jax.sharding import PartitionSpec as P

G = 32768
W = 8
TILE = 128
L_OUT = 1024
M_DEV = 16
U_START = 8192
V_START = 8192
V_WIN = 256
F32 = jnp.float32
BF16 = jnp.bfloat16
I32 = jnp.int32
NT = (((1,), (1,)), ((), ()))
SINE = [(-1) ** k * (2.0 * math.pi) ** (2 * k + 1) / math.factorial(2 * k + 1) for k in range(6)]


def quarter_sine(s):
    square = s * s
    total = jnp.full_like(s, SINE[5])
    for k in range(4, -1, -1):
        total = total * square + SINE[k]
    return total * s


def cos_turns(t):
    return quarter_sine(0.25 - jnp.abs(t))


def sin_turns(t):
    return quarter_sine(jnp.abs(jnp.abs(t - 0.25) - 0.5) - 0.25)


def wrap(turns):
    return (((turns + G // 2) & (G - 1)) - G // 2).astype(F32) * (1.0 / G)


def iota(shape, axis):
    return lax.broadcasted_iota(I32, shape, axis)


def pixel(index, step):
    return ((index * step) & (G - 1)) - G // 2


def taper(spread):
    return jnp.where(jnp.abs(spread) <= 4.0, jnp.exp(spread * spread * -0.125), 0.0)


def kernel(
    devices, cap, group, width, per_device,
    data_ref, w_ref, out_ref,
    key_s, send1, recv1, a_s, b_s, grid_s, tv_s, send2, recv2, tab_s, scr_c, scr_s, own_s, send3, recv3,
    ss1, rs1, ss2, rs2, ss3, rs3,
):
    me = lax.axis_index("row")
    blocks = devices // group
    m_step = G // (M_DEV * devices) + 1
    l_step = G // L_OUT + 1
    barrier = pltpu.get_barrier_semaphore()

    def greet(i, carry):
        pl.semaphore_signal(
            barrier, inc=1, device_id={"row": lax.rem(me + i, devices)},
            device_id_type=pl.DeviceIdType.MESH,
        )
        return carry

    lax.fori_loop(1, devices, greet, 0)

    def copy1(i):
        peer = lax.rem(me + i, devices)
        return pltpu.make_async_remote_copy(
            src_ref=send1.at[peer], dst_ref=recv1.at[me], send_sem=ss1.at[i], recv_sem=rs1.at[i],
            device_id={"row": peer}, device_id_type=pl.DeviceIdType.MESH,
        )

    def arrive1(i):
        source = lax.rem(me - i + devices, devices)
        return pltpu.make_async_remote_copy(
            src_ref=send1.at[source], dst_ref=recv1.at[source], send_sem=ss1.at[i], recv_sem=rs1.at[i],
            device_id={"row": source}, device_id_type=pl.DeviceIdType.MESH,
        )

    half = devices // 2
    core = lax.rem(me, 2)
    chip = me // 2
    partner = me + 1 - 2 * core
    swap = pltpu.make_async_remote_copy(
        src_ref=send2.at[pl.ds((1 - core) * half, half)], dst_ref=recv2, send_sem=ss2, recv_sem=rs2,
        device_id={"row": partner}, device_id_type=pl.DeviceIdType.MESH,
    )

    def copy3(i):
        there = lax.rem(chip + i, half)
        return pltpu.make_async_remote_copy(
            src_ref=send3.at[there], dst_ref=recv3.at[chip], send_sem=ss3.at[i], recv_sem=rs3.at[i],
            device_id={"row": there * 2 + core}, device_id_type=pl.DeviceIdType.MESH,
        )

    def arrive3(i):
        source = lax.rem(chip - i + half, half)
        return pltpu.make_async_remote_copy(
            src_ref=send3.at[source], dst_ref=recv3.at[source], send_sem=ss3.at[i], recv_sem=rs3.at[i],
            device_id={"row": source * 2 + core}, device_id_type=pl.DeviceIdType.MESH,
        )

    with jax.named_scope("pack"):
        data = data_ref[...]
        member = jnp.where(data[6:7, :] == iota((devices, per_device), 0).astype(F32), 1.0, 0.0)
        parts = [member[:, c * 128 : (c + 1) * 128] for c in range(per_device // 128)]
        below = jnp.where(iota((128, 128), 0) < iota((128, 128), 1), 1.0, 0.0).astype(BF16)
        ranks = jnp.dot(jnp.concatenate(parts, axis=0).astype(BF16), below, preferred_element_type=F32)
        before = jnp.zeros((devices, 1), F32) + lax.rem(me, group).astype(F32) * cap
        for c, part in enumerate(parts):
            rank = ranks[c * devices : (c + 1) * devices] + before
            key_s[:, c * 128 : (c + 1) * 128] = jnp.where(part > 0.0, rank, -1.0)
            before = before + jnp.sum(part, axis=1, keepdims=True)
        low = data.astype(BF16)

        def packed(d):
            slot = iota((width, per_device), 0).astype(F32)
            hot = jnp.where(slot == key_s[pl.ds(d, 1), :], 1.0, 0.0).astype(BF16)
            return lax.dot_general(low, hot, NT, preferred_element_type=F32)

        pl.semaphore_wait(barrier, devices - 1)

        def send_block(i, carry):
            d = lax.rem(me + i, devices)
            send1[d] = packed(d)
            copy1(i).start()
            return carry

        lax.fori_loop(1, devices, send_block, 0)
        recv1[me] = packed(me)

    with jax.named_scope("tables"):
        rows = 2 * M_DEV * devices
        tile_rows = 256

        def table_v(k, carry):
            row = iota((tile_rows, V_WIN), 0) + k * tile_rows
            place = row >> 5
            owner = jnp.where(place < half, place * 2, place * 2 + 1 - devices)
            part = (row >> 4) & 1
            om = pixel((row & 15) * devices + owner, m_step)
            turns = (iota((tile_rows, V_WIN), 1) + V_START) * om
            at = pl.ds(pl.multiple_of(k * tile_rows, tile_rows), tile_rows)
            tv_s[at, :V_WIN] = cos_turns(wrap(turns - part * (G // 4))).astype(BF16)
            tv_s[at, V_WIN:] = cos_turns(wrap(turns + (1 - part) * (G // 4))).astype(BF16)
            return carry

        lax.fori_loop(0, rows // tile_rows, table_v, 0)
        ol = pixel(iota((2 * TILE, L_OUT), 1), l_step)
        row_u = iota((2 * TILE, L_OUT), 0)
        along_u = U_START + jnp.where(row_u < TILE, row_u + me * TILE, row_u - TILE + partner * TILE)
        turn_u = wrap(along_u * ol)
        tab_s[:, :L_OUT] = cos_turns(turn_u).astype(BF16)
        tab_s[:, L_OUT:] = sin_turns(turn_u).astype(BF16)

    with jax.named_scope("screen"):

        def screen(there, carry):
            row = iota((M_DEV, L_OUT), 0) * devices + there * 2 + core
            y = pixel(row, m_step).astype(F32) * (1.0 / G)
            x = pixel(iota((M_DEV, L_OUT), 1), l_step).astype(F32) * (1.0 / G)
            q = x * x + y * y
            lowered = q / (1.0 + jnp.sqrt(1.0 - q))
            for p in range(W):
                turns = lowered * -w_ref[p]
                turns = turns - jnp.floor(turns + 0.5)
                scr_c[there, p] = cos_turns(turns)
                scr_s[there, p] = sin_turns(turns)
            return carry

        lax.fori_loop(0, half, screen, 0)

    def wait1(i, carry):
        arrive1(i).wait_recv()
        return carry

    lax.fori_loop(1, devices, wait1, 0)

    with jax.named_scope("spread"):

        def spread(k, carry):
            block = recv1[k * group]
            for j in range(1, group):
                block = block + recv1[k * group + j]
            at = pl.ds(pl.multiple_of(k * width, width), width)
            down = iota((TILE, width), 0).astype(F32)
            rows_k = taper(down - block[3:4, :]).astype(BF16)
            for p in range(W):
                mask = jnp.where(block[2:3, :] == p + 1.0, 1.0, 0.0).astype(BF16)
                b_s[p * TILE : (p + 1) * TILE, at] = rows_k * mask
            cols_k = taper(down - block[5:6, :])
            for e in range(2):
                for h in range(2):
                    value = jnp.where(block[4:5, :] == float(h), block[e : e + 1, :], 0.0)
                    first = e * V_WIN + h * TILE
                    a_s[first : first + TILE, at] = (cols_k * value).astype(BF16)
            return carry

        lax.fori_loop(0, blocks, spread, 0)

    with jax.named_scope("gridding"):

        def grid_tile(j, carry):
            at = pl.ds(pl.multiple_of(j * 256, 256), 256)
            grid_s[:, at] = lax.dot_general(a_s[...], b_s[at, :], NT, preferred_element_type=F32).astype(BF16)
            return carry

        lax.fori_loop(0, W * TILE // 256, grid_tile, 0)

    with jax.named_scope("columns"):

        def columns(k, first):
            start = first + k * (devices // 4)
            rows_k = 32 * (devices // 4)
            at = pl.ds(pl.multiple_of(start * 32, 32), rows_k)
            block = jnp.dot(tv_s[at, :], grid_s[...], preferred_element_type=F32).astype(BF16)
            for j in range(devices // 4):
                send2[start + j] = block[j * 32 : (j + 1) * 32]
            return first

        lax.fori_loop(0, 2, columns, (1 - core) * half)
        swap.start()
        lax.fori_loop(0, 2, columns, core * half)
        swap.wait_recv()

    with jax.named_scope("rows"):
        scale = 1.0 / math.sqrt(per_device * devices)

        def summand(there):
            for p in range(W):
                at = slice(p * TILE, (p + 1) * TILE)
                a_s[p * 32 : (p + 1) * 32, :TILE] = send2[core * half + there, :, at]
                a_s[p * 32 : (p + 1) * 32, TILE : 2 * TILE] = recv2[there, :, at]

            def image(k, carry):
                at = pl.ds(pl.multiple_of(k * 256, 256), 256)
                also = pl.ds(pl.multiple_of(k * 256 + L_OUT, 256), 256)
                left = a_s[: 32 * W, : 2 * TILE]
                by_cos = jnp.dot(left, tab_s[:, at], preferred_element_type=F32)
                by_sin = jnp.dot(left, tab_s[:, also], preferred_element_type=F32)
                total = jnp.zeros((M_DEV, 256), F32)
                for p in range(W):
                    r0, r1, r2 = p * 32, p * 32 + 16, p * 32 + 32
                    real = by_cos[r0:r1] - by_sin[r1:r2]
                    imag = by_sin[r0:r1] + by_cos[r1:r2]
                    total = total + scr_c[there, p, :, at] * real - scr_s[there, p, :, at] * imag
                own_s[:, at] = total * scale
                return carry

            lax.fori_loop(0, L_OUT // 256, image, 0, unroll=True)

        def send_summand(i, carry):
            there = lax.rem(chip + i, half)
            summand(there)
            send3[there] = own_s[...].astype(BF16)
            copy3(i).start()
            return carry

        lax.fori_loop(1, half, send_summand, 0)
        summand(chip)

        def add(i, carry):
            arrive3(i).wait_recv()
            own_s[...] += recv3[lax.rem(chip - i + half, half)].astype(F32)
            return carry

        lax.fori_loop(1, half, add, 0)
        out_ref[...] = own_s[...]

    def drain1(i, carry):
        copy1(i).wait_send()
        return carry

    def drain3(i, carry):
        copy3(i).wait_send()
        return carry

    lax.fori_loop(1, devices, drain1, 0)
    lax.fori_loop(1, half, drain3, 0)
    swap.wait_send()


def on_device(vis_values, tile_row, tile_col, row_offset, col_offset, plane, plane_w):
    devices = lax.axis_size("row")
    per_device = vis_values.shape[1]
    cap = 4 * per_device // devices
    group = max(1, 128 // cap)
    width = cap * group
    slots = width * (devices // group)
    ints = jnp.stack([plane + 1, row_offset, tile_col, col_offset, tile_row, jnp.zeros_like(plane)])
    data = jnp.concatenate([vis_values.astype(F32), ints.astype(F32)], axis=0)
    vmem = pl.BlockSpec(memory_space=pltpu.VMEM)
    return pl.pallas_call(
        functools.partial(kernel, devices, cap, group, width, per_device),
        out_shape=jax.ShapeDtypeStruct((M_DEV, L_OUT), F32),
        in_specs=[vmem, pl.BlockSpec(memory_space=pltpu.SMEM)],
        out_specs=vmem,
        scratch_shapes=[
            pltpu.VMEM((devices, per_device), F32),
            pltpu.VMEM((devices, 8, width), F32),
            pltpu.VMEM((devices, 8, width), F32),
            pltpu.VMEM((2 * V_WIN, slots), BF16),
            pltpu.VMEM((W * TILE, slots), BF16),
            pltpu.VMEM((2 * V_WIN, W * TILE), BF16),
            pltpu.VMEM((2 * M_DEV * devices, 2 * V_WIN), BF16),
            pltpu.VMEM((devices, 2 * M_DEV, W * TILE), BF16),
            pltpu.VMEM((devices // 2, 2 * M_DEV, W * TILE), BF16),
            pltpu.VMEM((2 * TILE, 2 * L_OUT), BF16),
            pltpu.VMEM((devices // 2, W, M_DEV, L_OUT), F32),
            pltpu.VMEM((devices // 2, W, M_DEV, L_OUT), F32),
            pltpu.VMEM((M_DEV, L_OUT), F32),
            pltpu.VMEM((devices // 2, M_DEV, L_OUT), BF16),
            pltpu.VMEM((devices // 2, M_DEV, L_OUT), BF16),
            pltpu.SemaphoreType.DMA((devices,)),
            pltpu.SemaphoreType.DMA((devices,)),
            pltpu.SemaphoreType.DMA,
            pltpu.SemaphoreType.DMA,
            pltpu.SemaphoreType.DMA((devices // 2,)),
            pltpu.SemaphoreType.DMA((devices // 2,)),
        ],
        compiler_params=pltpu.CompilerParams(
            collective_id=0, has_side_effects=True, vmem_limit_bytes=(40 if devices <= 16 else 62) * 2**20
        ),
    )(data, plane_w)


def solution(mesh):
    vector = P(("grp", "row"))
    in_specs = (P(None, ("grp", "row")), vector, vector, vector, vector, vector, P("grp"))
    return jax.shard_map(
        on_device, mesh=mesh, in_specs=in_specs, out_specs=P(("grp", "row"), None), check_vma=False
    )
```

```python
import functools
import math

import jax
import jax.numpy as jnp
from jax import lax
from jax.experimental import pallas as pl
from jax.experimental.pallas import tpu as pltpu
from jax.sharding import PartitionSpec as P

G = 32768
W = 8
TILE = 128
L_OUT = 1024
M_DEV = 16
U_START = 8192
V_START = 8192
V_WIN = 256
F32 = jnp.float32
BF16 = jnp.bfloat16
I32 = jnp.int32
NT = (((1,), (1,)), ((), ()))
SINE = [(-1) ** k * (2.0 * math.pi) ** (2 * k + 1) / math.factorial(2 * k + 1) for k in range(6)]


def quarter_sine(s):
    square = s * s
    total = jnp.full_like(s, SINE[5])
    for k in range(4, -1, -1):
        total = total * square + SINE[k]
    return total * s


def cos_turns(t):
    return quarter_sine(0.25 - jnp.abs(t))


def sin_turns(t):
    return quarter_sine(jnp.abs(jnp.abs(t - 0.25) - 0.5) - 0.25)


def wrap(turns):
    return (((turns + G // 2) & (G - 1)) - G // 2).astype(F32) * (1.0 / G)


def iota(shape, axis):
    return lax.broadcasted_iota(I32, shape, axis)


def pixel(index, step):
    return ((index * step) & (G - 1)) - G // 2


def taper(spread):
    return jnp.where(jnp.abs(spread) <= 4.0, jnp.exp(spread * spread * -0.125), 0.0)


def kernel(
    devices, cap, group, width, per_device,
    vis_ref, plane_ref, row_ref, tcol_ref, col_ref, trow_ref, w_ref, out_ref,
    ints_s, data_s, key_s, send1, recv1, a_s, b_s, grid_s, tv_s, send2, recv2, tab_s, scr_c, scr_s, own_s, send3, recv3,
    ss1, rs1, ss2, rs2, ss3, rs3, in_sem,
):
    me = lax.axis_index("row")
    blocks = devices // group
    m_step = G // (M_DEV * devices) + 1
    l_step = G // L_OUT + 1
    barrier = pltpu.get_barrier_semaphore()

    def greet(i, carry):
        pl.semaphore_signal(
            barrier, inc=1, device_id={"row": lax.rem(me + i, devices)},
            device_id_type=pl.DeviceIdType.MESH,
        )
        return carry

    inputs = (plane_ref, row_ref, tcol_ref, col_ref, trow_ref)
    fetches = [pltpu.make_async_copy(ref, ints_s.at[k], in_sem.at[k]) for k, ref in enumerate(inputs)]
    for fetch in fetches:
        fetch.start()
    lax.fori_loop(1, devices, greet, 0)
    for fetch in fetches:
        fetch.wait()

    def copy1(i):
        peer = lax.rem(me + i, devices)
        return pltpu.make_async_remote_copy(
            src_ref=send1.at[peer], dst_ref=recv1.at[me], send_sem=ss1.at[i], recv_sem=rs1.at[i],
            device_id={"row": peer}, device_id_type=pl.DeviceIdType.MESH,
        )

    def arrive1(i):
        source = lax.rem(me - i + devices, devices)
        return pltpu.make_async_remote_copy(
            src_ref=send1.at[source], dst_ref=recv1.at[source], send_sem=ss1.at[i], recv_sem=rs1.at[i],
            device_id={"row": source}, device_id_type=pl.DeviceIdType.MESH,
        )

    half = devices // 2
    core = lax.rem(me, 2)
    chip = me // 2
    partner = me + 1 - 2 * core
    swap = pltpu.make_async_remote_copy(
        src_ref=send2.at[pl.ds((1 - core) * half, half)], dst_ref=recv2, send_sem=ss2, recv_sem=rs2,
        device_id={"row": partner}, device_id_type=pl.DeviceIdType.MESH,
    )

    def copy3(i):
        there = lax.rem(chip + i, half)
        return pltpu.make_async_remote_copy(
            src_ref=send3.at[there], dst_ref=recv3.at[chip], send_sem=ss3.at[i], recv_sem=rs3.at[i],
            device_id={"row": there * 2 + core}, device_id_type=pl.DeviceIdType.MESH,
        )

    def arrive3(i):
        source = lax.rem(chip - i + half, half)
        return pltpu.make_async_remote_copy(
            src_ref=send3.at[source], dst_ref=recv3.at[source], send_sem=ss3.at[i], recv_sem=rs3.at[i],
            device_id={"row": source * 2 + core}, device_id_type=pl.DeviceIdType.MESH,
        )

    with jax.named_scope("pack"):
        data_s[0:2, :] = vis_ref[...].astype(F32)
        for c in range(per_device // 128):
            at = slice(c * 128, (c + 1) * 128)
            data_s[2:3, at] = ints_s[0, c : c + 1, :].astype(F32) + 1.0
            data_s[3:4, at] = ints_s[1, c : c + 1, :].astype(F32)
            data_s[4:5, at] = ints_s[2, c : c + 1, :].astype(F32)
            data_s[5:6, at] = ints_s[3, c : c + 1, :].astype(F32)
            data_s[6:7, at] = ints_s[4, c : c + 1, :].astype(F32)
        data_s[7:8, :] = jnp.zeros((1, per_device), F32)
        data = data_s[...]
        member = jnp.where(data[6:7, :] == iota((devices, per_device), 0).astype(F32), 1.0, 0.0)
        parts = [member[:, c * 128 : (c + 1) * 128] for c in range(per_device // 128)]
        below = jnp.where(iota((128, 128), 0) < iota((128, 128), 1), 1.0, 0.0).astype(BF16)
        ranks = jnp.dot(jnp.concatenate(parts, axis=0).astype(BF16), below, preferred_element_type=F32)
        before = jnp.zeros((devices, 1), F32) + lax.rem(me, group).astype(F32) * cap
        for c, part in enumerate(parts):
            rank = ranks[c * devices : (c + 1) * devices] + before
            key_s[:, c * 128 : (c + 1) * 128] = jnp.where(part > 0.0, rank, -1.0)
            before = before + jnp.sum(part, axis=1, keepdims=True)
        low = data.astype(BF16)

        def packed(d):
            slot = iota((width, per_device), 0).astype(F32)
            hot = jnp.where(slot == key_s[pl.ds(d, 1), :], 1.0, 0.0).astype(BF16)
            found = lax.dot_general(low, hot, NT, preferred_element_type=F32)
            second = found[:, 128:] if width > 128 else jnp.zeros((8, 128), F32)
            return jnp.concatenate([found[:, :128], second], axis=0).astype(BF16)

        pl.semaphore_wait(barrier, devices - 1)

        batch = 3 if (devices - 1) % 3 == 0 else 1

        def send_block(k, carry):
            steps = [k * batch + 1 + j for j in range(batch)]
            peers = [lax.rem(me + i, devices) for i in steps]
            found = [packed(d) for d in peers]
            for d, block in zip(peers, found):
                send1[d] = block
            for i in steps:
                copy1(i).start()
            return carry

        lax.fori_loop(0, (devices - 1) // batch, send_block, 0)
        recv1[me] = packed(me)

    with jax.named_scope("tables"):
        rows = 2 * M_DEV * devices
        tile_rows = 256

        def table_v(k, carry):
            row = iota((tile_rows, V_WIN), 0) + k * tile_rows
            place = row >> 5
            owner = jnp.where(place < half, place * 2, place * 2 + 1 - devices)
            part = (row >> 4) & 1
            om = pixel((row & 15) * devices + owner, m_step)
            turns = (iota((tile_rows, V_WIN), 1) + V_START) * om
            at = pl.ds(pl.multiple_of(k * tile_rows, tile_rows), tile_rows)
            tv_s[at, :V_WIN] = cos_turns(wrap(turns - part * (G // 4))).astype(BF16)
            tv_s[at, V_WIN:] = cos_turns(wrap(turns + (1 - part) * (G // 4))).astype(BF16)
            return carry

        lax.fori_loop(0, rows // tile_rows, table_v, 0)
        ol = pixel(iota((2 * TILE, L_OUT), 1), l_step)
        row_u = iota((2 * TILE, L_OUT), 0)
        along_u = U_START + jnp.where(row_u < TILE, row_u + me * TILE, row_u - TILE + partner * TILE)
        turn_u = wrap(along_u * ol)
        tab_s[:, :L_OUT] = cos_turns(turn_u).astype(BF16)
        tab_s[:, L_OUT:] = sin_turns(turn_u).astype(BF16)

    with jax.named_scope("screen"):

        def screen(there, carry):
            row = iota((M_DEV, L_OUT), 0) * devices + there * 2 + core
            y = pixel(row, m_step).astype(F32) * (1.0 / G)
            x = pixel(iota((M_DEV, L_OUT), 1), l_step).astype(F32) * (1.0 / G)
            q = x * x + y * y
            lowered = q / (1.0 + jnp.sqrt(1.0 - q))
            for p in range(W):
                turns = lowered * -w_ref[p]
                turns = turns - jnp.floor(turns + 0.5)
                scr_c[there, p] = cos_turns(turns)
                scr_s[there, p] = sin_turns(turns)
            return carry

        lax.fori_loop(0, half, screen, 0)

    def wait1(i, carry):
        arrive1(i).wait_recv()
        return carry

    lax.fori_loop(1, devices, wait1, 0)

    with jax.named_scope("spread"):

        def spread(k, carry):
            block = recv1[k * group].astype(F32)
            for j in range(1, group):
                block = block + recv1[k * group + j].astype(F32)
            block = jnp.concatenate([block[:8], block[8:]], axis=1)[:, :width]
            at = pl.ds(pl.multiple_of(k * width, width), width)
            down = iota((TILE, width), 0).astype(F32)
            rows_k = taper(down - block[3:4, :]).astype(BF16)
            for p in range(W):
                mask = jnp.where(block[2:3, :] == p + 1.0, 1.0, 0.0).astype(BF16)
                b_s[p * TILE : (p + 1) * TILE, at] = rows_k * mask
            cols_k = taper(down - block[5:6, :])
            for e in range(2):
                for h in range(2):
                    value = jnp.where(block[4:5, :] == float(h), block[e : e + 1, :], 0.0)
                    first = e * V_WIN + h * TILE
                    a_s[first : first + TILE, at] = (cols_k * value).astype(BF16)
            return carry

        lax.fori_loop(0, blocks, spread, 0, unroll=2)

    with jax.named_scope("gridding"):

        def grid_tile(j, carry):
            at = pl.ds(pl.multiple_of(j * 256, 256), 256)
            grid_s[:, at] = lax.dot_general(a_s[...], b_s[at, :], NT, preferred_element_type=F32).astype(BF16)
            return carry

        lax.fori_loop(0, W * TILE // 256, grid_tile, 0)

    with jax.named_scope("columns"):

        def columns(k, first):
            start = first + k * (devices // 4)
            rows_k = 32 * (devices // 4)
            at = pl.ds(pl.multiple_of(start * 32, 32), rows_k)
            block = jnp.dot(tv_s[at, :], grid_s[...], preferred_element_type=F32).astype(BF16)
            for j in range(devices // 4):
                send2[start + j] = block[j * 32 : (j + 1) * 32]
            return first

        lax.fori_loop(0, 2, columns, (1 - core) * half)
        swap.start()
        lax.fori_loop(0, 2, columns, core * half)
        swap.wait_recv()

    with jax.named_scope("rows"):
        scale = 1.0 / math.sqrt(per_device * devices)

        def summand(there):
            for p in range(W):
                at = slice(p * TILE, (p + 1) * TILE)
                a_s[p * 32 : (p + 1) * 32, :TILE] = send2[core * half + there, :, at]
                a_s[p * 32 : (p + 1) * 32, TILE : 2 * TILE] = recv2[there, :, at]

            def image(k, carry):
                at = pl.ds(pl.multiple_of(k * 256, 256), 256)
                also = pl.ds(pl.multiple_of(k * 256 + L_OUT, 256), 256)
                left = a_s[: 32 * W, : 2 * TILE]
                by_cos = jnp.dot(left, tab_s[:, at], preferred_element_type=F32)
                by_sin = jnp.dot(left, tab_s[:, also], preferred_element_type=F32)
                total = jnp.zeros((M_DEV, 256), F32)
                for p in range(W):
                    r0, r1, r2 = p * 32, p * 32 + 16, p * 32 + 32
                    real = by_cos[r0:r1] - by_sin[r1:r2]
                    imag = by_sin[r0:r1] + by_cos[r1:r2]
                    total = total + scr_c[there, p, :, at] * real - scr_s[there, p, :, at] * imag
                own_s[:, at] = total * scale
                return carry

            lax.fori_loop(0, L_OUT // 256, image, 0, unroll=True)

        def send_summand(i, carry):
            there = lax.rem(chip + i, half)
            summand(there)
            send3[there] = own_s[...].astype(BF16)
            copy3(i).start()
            return carry

        lax.fori_loop(1, half, send_summand, 0)
        summand(chip)

        def add(i, carry):
            arrive3(i).wait_recv()
            own_s[...] += recv3[lax.rem(chip - i + half, half)].astype(F32)
            return carry

        lax.fori_loop(1, half, add, 0)
        out_ref[...] = own_s[...]

    def drain1(i, carry):
        copy1(i).wait_send()
        return carry

    def drain3(i, carry):
        copy3(i).wait_send()
        return carry

    lax.fori_loop(1, devices, drain1, 0)
    lax.fori_loop(1, half, drain3, 0)
    swap.wait_send()


def on_device(vis_values, tile_row, tile_col, row_offset, col_offset, plane, plane_w):
    devices = lax.axis_size("row")
    per_device = vis_values.shape[1]
    cap = 4 * per_device // devices
    group = max(1, 128 // cap)
    width = cap * group
    slots = width * (devices // group)
    ints = [x.reshape(per_device // 128, 128) for x in (plane, row_offset, tile_col, col_offset, tile_row)]
    vmem = pl.BlockSpec(memory_space=pltpu.VMEM)
    return pl.pallas_call(
        functools.partial(kernel, devices, cap, group, width, per_device),
        out_shape=jax.ShapeDtypeStruct((M_DEV, L_OUT), F32),
        in_specs=[vmem] + [pl.BlockSpec(memory_space=pltpu.HBM)] * 5 + [pl.BlockSpec(memory_space=pltpu.SMEM)],
        out_specs=vmem,
        scratch_shapes=[
            pltpu.VMEM((5, per_device // 128, 128), I32),
            pltpu.VMEM((8, per_device), F32),
            pltpu.VMEM((devices, per_device), F32),
            pltpu.VMEM((devices, 16, 128), BF16),
            pltpu.VMEM((devices, 16, 128), BF16),
            pltpu.VMEM((2 * V_WIN, slots), BF16),
            pltpu.VMEM((W * TILE, slots), BF16),
            pltpu.VMEM((2 * V_WIN, W * TILE), BF16),
            pltpu.VMEM((2 * M_DEV * devices, 2 * V_WIN), BF16),
            pltpu.VMEM((devices, 2 * M_DEV, W * TILE), BF16),
            pltpu.VMEM((devices // 2, 2 * M_DEV, W * TILE), BF16),
            pltpu.VMEM((2 * TILE, 2 * L_OUT), BF16),
            pltpu.VMEM((devices // 2, W, M_DEV, L_OUT), F32),
            pltpu.VMEM((devices // 2, W, M_DEV, L_OUT), F32),
            pltpu.VMEM((M_DEV, L_OUT), F32),
            pltpu.VMEM((devices // 2, M_DEV, L_OUT), BF16),
            pltpu.VMEM((devices // 2, M_DEV, L_OUT), BF16),
            pltpu.SemaphoreType.DMA((devices,)),
            pltpu.SemaphoreType.DMA((devices,)),
            pltpu.SemaphoreType.DMA,
            pltpu.SemaphoreType.DMA,
            pltpu.SemaphoreType.DMA((devices // 2,)),
            pltpu.SemaphoreType.DMA((devices // 2,)),
            pltpu.SemaphoreType.DMA((5,)),
        ],
        compiler_params=pltpu.CompilerParams(
            collective_id=0, has_side_effects=True, vmem_limit_bytes=64 * 2**20
        ),
    )(vis_values, *ints, plane_w)


def solution(mesh):
    vector = P(("grp", "row"))
    in_specs = (P(None, ("grp", "row")), vector, vector, vector, vector, vector, P("grp"))
    return jax.shard_map(
        on_device, mesh=mesh, in_specs=in_specs, out_specs=P(("grp", "row"), None), check_vma=False
    )
```

```python
import functools
import math

import jax
import jax.numpy as jnp
from jax import lax
from jax.experimental import pallas as pl
from jax.experimental.pallas import tpu as pltpu
from jax.sharding import PartitionSpec as P

G = 32768
W = 8
TILE = 128
L_OUT = 1024
M_DEV = 16
U_START = 8192
V_START = 8192
V_WIN = 256
F32 = jnp.float32
BF16 = jnp.bfloat16
I32 = jnp.int32
NT = (((1,), (1,)), ((), ()))
SINE = [(-1) ** k * (2.0 * math.pi) ** (2 * k + 1) / math.factorial(2 * k + 1) for k in range(6)]


def quarter_sine(s):
    square = s * s
    total = jnp.full_like(s, SINE[5])
    for k in range(4, -1, -1):
        total = total * square + SINE[k]
    return total * s


def cos_turns(t):
    return quarter_sine(0.25 - jnp.abs(t))


def sin_turns(t):
    return quarter_sine(jnp.abs(jnp.abs(t - 0.25) - 0.5) - 0.25)


def wrap(turns):
    return (((turns + G // 2) & (G - 1)) - G // 2).astype(F32) * (1.0 / G)


def iota(shape, axis):
    return lax.broadcasted_iota(I32, shape, axis)


def pixel(index, step):
    return ((index * step) & (G - 1)) - G // 2


def taper(spread):
    return jnp.where(jnp.abs(spread) <= 4.0, jnp.exp(spread * spread * -0.125), 0.0)


def kernel(
    devices, cap, group, width, per_device,
    vis_ref, plane_ref, row_ref, tcol_ref, col_ref, trow_ref, w_ref, out_ref,
    ints_s, data_s, key_s, send1, recv1, a_s, b_s, grid_s, tv_s, send2, recv2, tab_s, scr_c, scr_s, own_s, send3, recv3,
    ss1, rs1, ss2, rs2, ss3, rs3, in_sem,
):
    me = lax.axis_index("row")
    blocks = devices // group
    m_step = G // (M_DEV * devices) + 1
    l_step = G // L_OUT + 1
    barrier = pltpu.get_barrier_semaphore()

    def greet(i, carry):
        pl.semaphore_signal(
            barrier, inc=1, device_id={"row": lax.rem(me + i, devices)},
            device_id_type=pl.DeviceIdType.MESH,
        )
        return carry

    inputs = (plane_ref, row_ref, tcol_ref, col_ref, trow_ref)
    fetches = [pltpu.make_async_copy(ref, ints_s.at[k], in_sem.at[k]) for k, ref in enumerate(inputs)]
    for fetch in fetches:
        fetch.start()
    lax.fori_loop(1, devices, greet, 0)
    for fetch in fetches:
        fetch.wait()

    def copy1(i):
        peer = lax.rem(me + i, devices)
        return pltpu.make_async_remote_copy(
            src_ref=send1.at[peer], dst_ref=recv1.at[me], send_sem=ss1.at[i], recv_sem=rs1.at[i],
            device_id={"row": peer}, device_id_type=pl.DeviceIdType.MESH,
        )

    def arrive1(i):
        source = lax.rem(me - i + devices, devices)
        return pltpu.make_async_remote_copy(
            src_ref=send1.at[source], dst_ref=recv1.at[source], send_sem=ss1.at[i], recv_sem=rs1.at[i],
            device_id={"row": source}, device_id_type=pl.DeviceIdType.MESH,
        )

    half = devices // 2
    core = lax.rem(me, 2)
    chip = me // 2
    partner = me + 1 - 2 * core
    swap = pltpu.make_async_remote_copy(
        src_ref=send2.at[pl.ds((1 - core) * half, half)], dst_ref=recv2, send_sem=ss2, recv_sem=rs2,
        device_id={"row": partner}, device_id_type=pl.DeviceIdType.MESH,
    )

    def copy3(i):
        there = lax.rem(chip + i, half)
        return pltpu.make_async_remote_copy(
            src_ref=send3.at[there], dst_ref=recv3.at[chip], send_sem=ss3.at[i], recv_sem=rs3.at[i],
            device_id={"row": there * 2 + core}, device_id_type=pl.DeviceIdType.MESH,
        )

    def arrive3(i):
        source = lax.rem(chip - i + half, half)
        return pltpu.make_async_remote_copy(
            src_ref=send3.at[source], dst_ref=recv3.at[source], send_sem=ss3.at[i], recv_sem=rs3.at[i],
            device_id={"row": source * 2 + core}, device_id_type=pl.DeviceIdType.MESH,
        )

    with jax.named_scope("pack"):
        data_s[0:2, :] = vis_ref[...].astype(F32)
        for c in range(per_device // 128):
            at = slice(c * 128, (c + 1) * 128)
            data_s[2:3, at] = ints_s[0, c : c + 1, :].astype(F32) + 1.0
            data_s[3:4, at] = ints_s[1, c : c + 1, :].astype(F32)
            data_s[4:5, at] = ints_s[2, c : c + 1, :].astype(F32)
            data_s[5:6, at] = ints_s[3, c : c + 1, :].astype(F32)
            data_s[6:7, at] = ints_s[4, c : c + 1, :].astype(F32)
        data_s[7:8, :] = jnp.zeros((1, per_device), F32)
        data = data_s[...]
        member = jnp.where(data[6:7, :] == iota((devices, per_device), 0).astype(F32), 1.0, 0.0)
        parts = [member[:, c * 128 : (c + 1) * 128] for c in range(per_device // 128)]
        below = jnp.where(iota((128, 128), 0) < iota((128, 128), 1), 1.0, 0.0).astype(BF16)
        ranks = jnp.dot(jnp.concatenate(parts, axis=0).astype(BF16), below, preferred_element_type=F32)
        before = jnp.zeros((devices, 1), F32) + lax.rem(me, group).astype(F32) * cap
        for c, part in enumerate(parts):
            rank = ranks[c * devices : (c + 1) * devices] + before
            key_s[:, c * 128 : (c + 1) * 128] = jnp.where(part > 0.0, rank, -1.0)
            before = before + jnp.sum(part, axis=1, keepdims=True)
        low = data.astype(BF16)

        def packed(d):
            slot = iota((width, per_device), 0).astype(F32)
            hot = jnp.where(slot == key_s[pl.ds(d, 1), :], 1.0, 0.0).astype(BF16)
            found = lax.dot_general(low, hot, NT, preferred_element_type=F32)
            second = found[:, 128:] if width > 128 else jnp.zeros((8, 128), F32)
            return jnp.concatenate([found[:, :128], second], axis=0).astype(BF16)

        pl.semaphore_wait(barrier, devices - 1)

        batch = 3 if (devices - 1) % 3 == 0 else 1

        def send_block(k, carry):
            steps = [k * batch + 1 + j for j in range(batch)]
            peers = [lax.rem(me + i, devices) for i in steps]
            found = [packed(d) for d in peers]
            for d, block in zip(peers, found):
                send1[d] = block
            for i in steps:
                copy1(i).start()
            return carry

        lax.fori_loop(0, (devices - 1) // batch, send_block, 0)
        recv1[me] = packed(me)

    with jax.named_scope("tables"):
        rows = 2 * M_DEV * devices
        tile_rows = 256

        def table_v(k, carry):
            row = iota((tile_rows, V_WIN), 0) + k * tile_rows
            place = row >> 5
            owner = jnp.where(place < half, place * 2, place * 2 + 1 - devices)
            part = (row >> 4) & 1
            om = pixel((row & 15) * devices + owner, m_step)
            turns = (iota((tile_rows, V_WIN), 1) + V_START) * om
            at = pl.ds(pl.multiple_of(k * tile_rows, tile_rows), tile_rows)
            tv_s[at, :V_WIN] = cos_turns(wrap(turns - part * (G // 4))).astype(BF16)
            tv_s[at, V_WIN:] = cos_turns(wrap(turns + (1 - part) * (G // 4))).astype(BF16)
            return carry

        lax.fori_loop(0, rows // tile_rows, table_v, 0)
        ol = pixel(iota((2 * TILE, L_OUT), 1), l_step)
        row_u = iota((2 * TILE, L_OUT), 0)
        along_u = U_START + jnp.where(row_u < TILE, row_u + me * TILE, row_u - TILE + partner * TILE)
        turn_u = wrap(along_u * ol)
        tab_s[:, :L_OUT] = cos_turns(turn_u).astype(BF16)
        tab_s[:, L_OUT:] = sin_turns(turn_u).astype(BF16)

    with jax.named_scope("screen"):

        def screen(there, carry):
            row = iota((M_DEV, L_OUT), 0) * devices + there * 2 + core
            y = pixel(row, m_step).astype(F32) * (1.0 / G)
            x = pixel(iota((M_DEV, L_OUT), 1), l_step).astype(F32) * (1.0 / G)
            q = x * x + y * y
            lowered = q / (1.0 + jnp.sqrt(1.0 - q))
            for p in range(W):
                turns = lowered * -w_ref[p]
                turns = turns - jnp.floor(turns + 0.5)
                scr_c[there, p] = cos_turns(turns)
                scr_s[there, p] = sin_turns(turns)
            return carry

        early = half - half // 4
        lax.fori_loop(0, early, screen, 0)

    def wait1(i, carry):
        arrive1(i).wait_recv()
        return carry

    lax.fori_loop(1, devices, wait1, 0)

    with jax.named_scope("spread"):

        def spread(k, carry):
            block = recv1[k * group].astype(F32)
            for j in range(1, group):
                block = block + recv1[k * group + j].astype(F32)
            block = jnp.concatenate([block[:8], block[8:]], axis=1)[:, :width]
            at = pl.ds(pl.multiple_of(k * width, width), width)
            down = iota((TILE, width), 0).astype(F32)
            rows_k = taper(down - block[3:4, :]).astype(BF16)
            for p in range(W):
                mask = jnp.where(block[2:3, :] == p + 1.0, 1.0, 0.0).astype(BF16)
                b_s[p * TILE : (p + 1) * TILE, at] = rows_k * mask
            cols_k = taper(down - block[5:6, :])
            for e in range(2):
                for h in range(2):
                    value = jnp.where(block[4:5, :] == float(h), block[e : e + 1, :], 0.0)
                    first = e * V_WIN + h * TILE
                    a_s[first : first + TILE, at] = (cols_k * value).astype(BF16)
            return carry

        lax.fori_loop(0, blocks, spread, 0, unroll=2)

    with jax.named_scope("gridding"):

        def grid_tile(j, carry):
            at = pl.ds(pl.multiple_of(j * 256, 256), 256)
            grid_s[:, at] = lax.dot_general(a_s[...], b_s[at, :], NT, preferred_element_type=F32).astype(BF16)
            return carry

        lax.fori_loop(0, W * TILE // 256, grid_tile, 0)

    with jax.named_scope("columns"):

        def columns(k, first):
            start = first + k * (devices // 4)
            rows_k = 32 * (devices // 4)
            at = pl.ds(pl.multiple_of(start * 32, 32), rows_k)
            block = jnp.dot(tv_s[at, :], grid_s[...], preferred_element_type=F32).astype(BF16)
            for j in range(devices // 4):
                send2[start + j] = block[j * 32 : (j + 1) * 32]
            return first

        lax.fori_loop(0, 2, columns, (1 - core) * half)
        swap.start()
        lax.fori_loop(0, 2, columns, core * half)
        lax.fori_loop(early, half, screen, 0)
        swap.wait_recv()

    with jax.named_scope("rows"):
        scale = 1.0 / math.sqrt(per_device * devices)

        def summand(there):
            for p in range(W):
                at = slice(p * TILE, (p + 1) * TILE)
                a_s[p * 32 : (p + 1) * 32, :TILE] = send2[core * half + there, :, at]
                a_s[p * 32 : (p + 1) * 32, TILE : 2 * TILE] = recv2[there, :, at]

            def image(k, carry):
                at = pl.ds(pl.multiple_of(k * 256, 256), 256)
                also = pl.ds(pl.multiple_of(k * 256 + L_OUT, 256), 256)
                left = a_s[: 32 * W, : 2 * TILE]
                by_cos = jnp.dot(left, tab_s[:, at], preferred_element_type=F32)
                by_sin = jnp.dot(left, tab_s[:, also], preferred_element_type=F32)
                total = jnp.zeros((M_DEV, 256), F32)
                for p in range(W):
                    r0, r1, r2 = p * 32, p * 32 + 16, p * 32 + 32
                    real = by_cos[r0:r1] - by_sin[r1:r2]
                    imag = by_sin[r0:r1] + by_cos[r1:r2]
                    total = total + scr_c[there, p, :, at] * real - scr_s[there, p, :, at] * imag
                own_s[:, at] = total * scale
                return carry

            lax.fori_loop(0, L_OUT // 256, image, 0, unroll=True)

        def send_summand(i, carry):
            there = lax.rem(chip + i, half)
            summand(there)
            send3[there] = own_s[...].astype(BF16)
            copy3(i).start()
            return carry

        lax.fori_loop(1, half, send_summand, 0)
        summand(chip)

        def add(i, carry):
            arrive3(i).wait_recv()
            own_s[...] += recv3[lax.rem(chip - i + half, half)].astype(F32)
            return carry

        lax.fori_loop(1, half, add, 0)
        out_ref[...] = own_s[...]

    def drain1(i, carry):
        copy1(i).wait_send()
        return carry

    def drain3(i, carry):
        copy3(i).wait_send()
        return carry

    lax.fori_loop(1, devices, drain1, 0)
    lax.fori_loop(1, half, drain3, 0)
    swap.wait_send()


def on_device(vis_values, tile_row, tile_col, row_offset, col_offset, plane, plane_w):
    devices = lax.axis_size("row")
    per_device = vis_values.shape[1]
    cap = 4 * per_device // devices
    group = max(1, 128 // cap)
    width = cap * group
    slots = width * (devices // group)
    ints = [x.reshape(per_device // 128, 128) for x in (plane, row_offset, tile_col, col_offset, tile_row)]
    vmem = pl.BlockSpec(memory_space=pltpu.VMEM)
    return pl.pallas_call(
        functools.partial(kernel, devices, cap, group, width, per_device),
        out_shape=jax.ShapeDtypeStruct((M_DEV, L_OUT), F32),
        in_specs=[vmem] + [pl.BlockSpec(memory_space=pltpu.HBM)] * 5 + [pl.BlockSpec(memory_space=pltpu.SMEM)],
        out_specs=vmem,
        scratch_shapes=[
            pltpu.VMEM((5, per_device // 128, 128), I32),
            pltpu.VMEM((8, per_device), F32),
            pltpu.VMEM((devices, per_device), F32),
            pltpu.VMEM((devices, 16, 128), BF16),
            pltpu.VMEM((devices, 16, 128), BF16),
            pltpu.VMEM((2 * V_WIN, slots), BF16),
            pltpu.VMEM((W * TILE, slots), BF16),
            pltpu.VMEM((2 * V_WIN, W * TILE), BF16),
            pltpu.VMEM((2 * M_DEV * devices, 2 * V_WIN), BF16),
            pltpu.VMEM((devices, 2 * M_DEV, W * TILE), BF16),
            pltpu.VMEM((devices // 2, 2 * M_DEV, W * TILE), BF16),
            pltpu.VMEM((2 * TILE, 2 * L_OUT), BF16),
            pltpu.VMEM((devices // 2, W, M_DEV, L_OUT), F32),
            pltpu.VMEM((devices // 2, W, M_DEV, L_OUT), F32),
            pltpu.VMEM((M_DEV, L_OUT), F32),
            pltpu.VMEM((devices // 2, M_DEV, L_OUT), BF16),
            pltpu.VMEM((devices // 2, M_DEV, L_OUT), BF16),
            pltpu.SemaphoreType.DMA((devices,)),
            pltpu.SemaphoreType.DMA((devices,)),
            pltpu.SemaphoreType.DMA,
            pltpu.SemaphoreType.DMA,
            pltpu.SemaphoreType.DMA((devices // 2,)),
            pltpu.SemaphoreType.DMA((devices // 2,)),
            pltpu.SemaphoreType.DMA((5,)),
        ],
        compiler_params=pltpu.CompilerParams(
            collective_id=0, has_side_effects=True, vmem_limit_bytes=64 * 2**20
        ),
    )(vis_values, *ints, plane_w)


def solution(mesh):
    vector = P(("grp", "row"))
    in_specs = (P(None, ("grp", "row")), vector, vector, vector, vector, vector, P("grp"))
    return jax.shard_map(
        on_device, mesh=mesh, in_specs=in_specs, out_specs=P(("grp", "row"), None), check_vma=False
    )
```
